512 devices in a mesh: row: 16 (over z_hi, y), col: 32 (over z_lo, x, core).
Axes of the slice: x: 4, y: 4, z: 16 (z_hi: 4, z_lo: 4; z = z_hi * 4 + z_lo), core: 2. Of those that a mesh axis runs over, the one named last changes fastest.
Arguments:
- features: bfloat16 [16, 32, 128, 128], P('row', 'col'), may hold values from -6 to 6
- adjacency: bfloat16 [16, 32, 128, 128, 128], P('row', 'col'), may hold values from -0.059814453 to 0.059814453
- block_rows: int32 [16, 32, 128], P('row', 'col'), may hold values from 0 to 31
- block_cols: int32 [16, 32, 128], P('row', 'col'), may hold values from 0 to 15
- counts: int32 [16, 32], P('row', 'col'), may hold values from 32 to 128, as said below
- weights: bfloat16 [2, 128, 128], replicated, may hold values from -0.5 to 0.5
Outputs:
- embedded: bfloat16 [16, 32, 128, 128], P('row', 'col')
The draws below stay inside these ranges and needn't reach their ends.
Inputs may be any that keep to these rules, and one draw needn't show every extreme that they name: Slots from counts on are unused; some tile uses all 128 slots.
All inputs are finite; a program needn't handle non-finite values.
Results may differ from the reference program's by a relative error of at most 0.009.
Values may be sent and summed in bfloat16 or wider, within the bound.
A program may use at most 64 MiB of HBM per device.

```python
import jax
import jax.numpy as jnp
from jax import lax

F = 128
BLOCK = 128
SLOTS = 128
LAYERS = 2
ROW_GROUPS = 16
COL_GROUPS = 32


def draw_counts(key, part):
    key = jax.random.fold_in(key, 7)
    key_base, key_pick = jax.random.split(key)
    counts = jax.random.randint(key_base, (ROW_GROUPS * COL_GROUPS,), SLOTS // 4, SLOTS + 1)
    chosen = jax.random.randint(key_pick, (), 0, ROW_GROUPS * COL_GROUPS)
    counts = jnp.where(jnp.arange(ROW_GROUPS * COL_GROUPS) == chosen, SLOTS, counts)
    return counts.reshape(ROW_GROUPS, COL_GROUPS).astype(jnp.int32)


def touch_ends(array, own_key, smallest, largest):
    index_at = [jax.random.randint(jax.random.fold_in(own_key, axis), (), 0, length) for axis, length in enumerate(array.shape)]
    main_axis = array.shape.index(max(array.shape))
    beside = index_at[:main_axis] + [(index_at[main_axis] + 1) % array.shape[main_axis]] + index_at[main_axis + 1:]
    return array.at[tuple(index_at)].set(smallest).at[tuple(beside)].set(largest)


def level_of(own_key, shape, cuts, least, top_value):
    gain = 1.0
    for axis_at, shards_of in cuts:
        draws = jax.random.uniform(jax.random.fold_in(jax.random.fold_in(own_key, 6), axis_at), (shards_of,), jnp.float32, least / len(cuts), top_value / len(cuts))
        gain = gain * jnp.repeat(jnp.exp(draws), shape[axis_at] // shards_of).reshape((-1,) + (1,) * (len(shape) - 1 - axis_at))
    return gain


def bell_draw(key, dims, scale, bound, cuts=(), kind=jnp.bfloat16):
    entries = jax.random.normal(key, dims, jnp.float32) * scale
    if len(cuts) > 0:
        entries = level_of(key, dims, cuts, -0.22, 0.18) * entries
    return jnp.clip(entries, min=-bound, max=bound).astype(kind)


def setup_inputs(seed: int = 0) -> dict:
    streams_of = jax.random.split(jax.random.key(seed), 7)
    features = bell_draw(streams_of[0], (ROW_GROUPS, COL_GROUPS, BLOCK, F), 1.0, 6.0, ((0, 16), (1, 32)))
    adjacency = bell_draw(streams_of[1], (ROW_GROUPS, COL_GROUPS, SLOTS, BLOCK, BLOCK), 0.01, 0.059814453, ((0, 16), (1, 32)))
    block_rows = touch_ends(jax.random.randint(streams_of[2], (ROW_GROUPS, COL_GROUPS, SLOTS), 0, COL_GROUPS), jax.random.fold_in(streams_of[2], 1), 0, COL_GROUPS - 1).astype(jnp.int32)
    block_cols = touch_ends(jax.random.randint(streams_of[3], (ROW_GROUPS, COL_GROUPS, SLOTS), 0, ROW_GROUPS), jax.random.fold_in(streams_of[3], 1), 0, ROW_GROUPS - 1).astype(jnp.int32)
    counts = draw_counts(jax.random.fold_in(streams_of[6], 71), 0)
    weights = bell_draw(streams_of[5], (LAYERS, F, F), F ** -0.5, 0.5)
    return dict(features=features, adjacency=adjacency, block_rows=block_rows, block_cols=block_cols, counts=counts, weights=weights)


def tile_partial(blocks, rows, cols, count, source):
    picked = source[cols].astype(jnp.float32)
    products = jnp.einsum("kij,kjf->kif", blocks.astype(jnp.float32), picked, precision=lax.Precision.HIGHEST)
    live_slots = (jnp.arange(SLOTS, dtype=jnp.int32) < count).astype(jnp.float32)
    row_hot = (rows[None, :] == jnp.arange(COL_GROUPS, dtype=jnp.int32)[:, None]).astype(jnp.float32) * live_slots[None, :]
    return jnp.dot(row_hot, products.reshape(SLOTS, BLOCK * F), precision=lax.Precision.HIGHEST)


def reference(features, adjacency, block_rows, block_cols, counts, weights):
    current = features
    for layer_index in range(LAYERS):
        def one_row(row_index):
            def step(total, col_index):
                partial_value = tile_partial(adjacency[row_index, col_index], block_rows[row_index, col_index], block_cols[row_index, col_index], counts[row_index, col_index], current[:, col_index])
                return total + partial_value, None
            total, unused = lax.scan(step, jnp.zeros((COL_GROUPS, BLOCK * F), jnp.float32), jnp.arange(COL_GROUPS, dtype=jnp.int32))
            return total
        summed = lax.map(one_row, jnp.arange(ROW_GROUPS, dtype=jnp.int32))
        aggregated = summed.reshape(ROW_GROUPS * COL_GROUPS * BLOCK, F).astype(jnp.bfloat16)
        hidden = jnp.dot(aggregated, weights[layer_index], preferred_element_type=jnp.float32)
        if layer_index + 1 < LAYERS:
            hidden = jax.nn.relu(hidden)
        current = hidden.astype(jnp.bfloat16).reshape(ROW_GROUPS, COL_GROUPS, BLOCK, F)
    return current
```

```python
import functools

import jax
import jax.numpy as jnp
from jax import lax
from jax.experimental import pallas as pl
from jax.experimental.pallas import tpu as pltpu
from jax.sharding import PartitionSpec as P

LAYERS = 2
BLOCK = 128
HALF = 64
ROWS = 16
PAIRS = 80
UNROLL = 4
DZ_ORDER = (2, 1, 3, 0)
DX_ORDER = (2, 1, 3, 0)
MESH = pl.DeviceIdType.MESH


def turned(vector):
    return jnp.transpose(jnp.broadcast_to(vector, (BLOCK, BLOCK)))


def slot_table(rows, cols, count):
    lane = lax.broadcasted_iota(jnp.int32, (BLOCK, BLOCK), 1)
    sub = lax.broadcasted_iota(jnp.int32, (BLOCK, BLOCK), 0)
    one = lane[:1]
    live = one < count
    rows = jnp.where(live, rows, BLOCK)
    rows_b = jnp.broadcast_to(rows, (BLOCK, BLOCK))
    rows_t = turned(rows)
    rank = jnp.sum(((rows_b == rows_t) & (sub < lane)).astype(jnp.int32), axis=0, keepdims=True)
    sizes = jnp.sum((rows_t == lane).astype(jnp.int32), axis=0, keepdims=True)
    pairs = turned((sizes + 1) >> 1)
    firsts = jnp.sum(jnp.where(sub < lane, pairs, 0), axis=0, keepdims=True)
    before = jnp.sum(jnp.where(sub < rows_b, pairs, 0), axis=0, keepdims=True)
    place = jnp.where(live, 2 * before + rank, 4 * BLOCK)
    packed = turned(place * 4096 + cols * BLOCK + one)
    place_t = packed >> 12
    value = (packed & 4095) - ROWS * BLOCK
    tables = [
        jnp.sum(jnp.where(place_t == lane + base, value, 0), axis=0, keepdims=True) + ROWS * BLOCK
        for base in (0, BLOCK)
    ]
    return firsts, tables[0], tables[1]


def kernel(
    feat_hbm, adj_hbm, rows_hbm, cols_hbm, count_hbm, weight_hbm, out_ref,
    adj, rows_v, cols_v, count_v, weight_v, held_0, held_1, prefix, table_v, table_s,
    send_c, recv_c, send_x, recv_x, send_m, recv_m, send_z, recv_z,
    local_sem, gs_sem, gr_sem, cs_sem, cr_sem, xs_sem, xr_sem, ms_sem, mr_sem, zs_sem, zr_sem,
):
    row, col = lax.axis_index("row"), lax.axis_index("col")
    zh, y = row // 4, row % 4
    zl, x, core = col // 8, (col // 2) % 4, col % 2

    def at_row(dz, dy):
        return ((zh + dz) % 4) * 4 + (y + dy) % 4

    def at_col(dz, dx, other):
        side = 1 - core if other else core
        return ((zl + dz) % 4) * 8 + ((x + dx) % 4) * 2 + side

    z_up, z_down = (at_row(1, 0), col), (at_row(3, 0), col)
    y_up, y_down = (at_row(0, 1), col), (at_row(0, 3), col)
    sibling = (row, at_col(0, 0, True))
    x_up, x_down = (row, at_col(0, 1, False)), (row, at_col(0, 3, False))
    peers = {dz: (row, at_col(dz, 0, False)) for dz in (1, 2, 3)}

    helds = (held_0, held_1)
    loads = [
        pltpu.make_async_copy(source, target, local_sem.at[at])
        for at, (source, target) in enumerate((
            (rows_hbm, rows_v), (cols_hbm, cols_v), (count_hbm, count_v),
            (feat_hbm, held_0.at[row]), (weight_hbm, weight_v), (adj_hbm, adj),
        ))
    ]
    for load in loads:
        load.start()

    barrier = pltpu.get_barrier_semaphore()
    partners = [z_up, z_down, y_up, y_down, sibling, x_up, x_down] + list(peers.values())
    for partner in partners:
        pl.semaphore_signal(barrier, inc=1, device_id=partner, device_id_type=MESH)
    for held in helds:
        held[ROWS] = jnp.zeros((BLOCK, BLOCK), jnp.bfloat16)
    prefix[0] = jnp.zeros((BLOCK, BLOCK), jnp.float32)
    pl.semaphore_wait(barrier, len(partners))

    sent = []

    def push(src, dst, send_sem, recv_sem, device):
        copy = pltpu.make_async_remote_copy(
            src_ref=src, dst_ref=dst, send_sem=send_sem, recv_sem=recv_sem,
            device_id=device, device_id_type=MESH,
        )
        copy.start()
        sent.append(copy)

    def await_into(dst, recv_sem):
        pltpu.make_async_remote_copy(
            src_ref=dst, dst_ref=dst, send_sem=recv_sem, recv_sem=recv_sem,
            device_id=sibling, device_id_type=MESH,
        ).wait_recv()

    for layer in range(LAYERS):
        count = [0]
        held = helds[layer]

        def half_of(origin, half):
            return held.at[origin, pl.ds(half * HALF, HALF)]

        def give(dz, dy, half, device):
            origin = at_row(dz, dy)
            source = half_of(origin, half)
            if layer == 0 and dz == 0 and dy == 0:
                source = feat_hbm.at[pl.ds(half * HALF, HALF)]
            push(
                source, half_of(origin, half),
                gs_sem.at[layer, count[0]], gr_sem.at[layer, 2 * origin + half], device,
            )
            count[0] += 1

        def take(dz, dy, half):
            origin = at_row(dz, dy)
            await_into(half_of(origin, half), gr_sem.at[layer, 2 * origin + half])

        def spread(dz, half):
            give(dz, 0, half, y_up if half == 0 else y_down)
            give(dz, 0, half, y_down if half == 0 else y_up)

        def relay_y(dz):
            take(dz, 3, 0)
            give(dz, 3, 0, y_up)
            take(dz, 1, 1)
            give(dz, 1, 1, y_down)

        give(0, 0, 0, z_up)
        give(0, 0, 1, z_down)
        give(0, 0, 1, z_up)
        give(0, 0, 0, z_down)
        spread(0, 0)
        spread(0, 1)

        if layer == 0:
            for load in loads[:3]:
                load.wait()
            firsts, low, high = slot_table(rows_v[...], cols_v[...], count_v[...])
            table_v[0:1] = firsts
            table_v[1:2] = low
            table_v[2:3] = high
            to_scalar = pltpu.make_async_copy(table_v, table_s, local_sem.at[6])
            to_scalar.start()

        relay_y(0)
        take(3, 0, 0)
        give(3, 0, 0, z_up)
        take(1, 0, 1)
        give(1, 0, 1, z_down)
        spread(3, 0)
        spread(1, 1)
        take(3, 0, 1)
        spread(3, 1)
        take(1, 0, 0)
        spread(1, 0)
        relay_y(3)
        relay_y(1)
        take(2, 0, 0)
        spread(2, 0)
        take(2, 0, 1)
        spread(2, 1)
        relay_y(2)
        for dz in (0, 3, 1, 2):
            take(dz, 3, 1)
            take(dz, 1, 0)
            take(dz, 2, 0)
            take(dz, 2, 1)

        if layer == 0:
            to_scalar.wait()
            for load in loads[3:]:
                load.wait()

        def pair_step(step, total):
            for part in range(UNROLL):
                pair = step * UNROLL + part
                line = 1 + pair // 64
                first = table_s[line, (2 * pair) % BLOCK]
                second = table_s[line, (2 * pair) % BLOCK + 1]
                left = jnp.concatenate([adj[first & 127], adj[second & 127]], axis=1)
                right = jnp.concatenate([held[first >> 7], held[second >> 7]], axis=0)
                total = total + jnp.dot(left, right, preferred_element_type=jnp.float32)
                prefix[pair + 1] = total
            return total

        lax.fori_loop(0, PAIRS // UNROLL, pair_step, jnp.zeros((BLOCK, BLOCK), jnp.float32))

        def partial(dz, dx, other, low=0, size=BLOCK):
            index = at_col(dz, dx, other)
            first, last = table_s[0, index], table_s[0, index + 1]
            span = pl.ds(low, size)
            return prefix[last, span] - prefix[first, span]

        def own(dz, dx, low=0, size=BLOCK):
            from_sibling = recv_c[layer, dz, dx, pl.ds(low, size)].astype(jnp.float32)
            return partial(dz, dx, False, low, size) + from_sibling

        def stage_core(dz):
            for dx in DX_ORDER:
                send_c[layer, dz, dx] = partial(dz, dx, True).astype(jnp.bfloat16)
            push(
                send_c.at[layer, dz], recv_c.at[layer, dz],
                cs_sem.at[layer, dz], cr_sem.at[layer, dz], sibling,
            )

        def stage_far(dz):
            await_into(recv_c.at[layer, dz], cr_sem.at[layer, dz])
            across = own(dz, 2).astype(jnp.bfloat16)
            send_x[layer, dz, 0, 0:HALF] = across[:HALF]
            send_x[layer, dz, 1, 0:HALF] = across[HALF:]
            send_x[layer, dz, 0, HALF:BLOCK] = own(dz, 1, HALF, HALF).astype(jnp.bfloat16)
            send_x[layer, dz, 1, HALF:BLOCK] = own(dz, 3, 0, HALF).astype(jnp.bfloat16)
            for way, device in ((0, x_up), (1, x_down)):
                push(
                    send_x.at[layer, dz, way], recv_x.at[layer, dz, way],
                    xs_sem.at[layer, dz, way], xr_sem.at[layer, dz, way], device,
                )

        def stage_near(dz):
            for way, dx, low, device in ((0, 1, 0, x_up), (1, 3, HALF, x_down)):
                await_into(recv_x.at[layer, dz, way], xr_sem.at[layer, dz, way])
                relayed = recv_x[layer, dz, way, 0:HALF].astype(jnp.float32)
                send_m[layer, dz, way] = (own(dz, dx, low, HALF) + relayed).astype(jnp.bfloat16)
                push(
                    send_m.at[layer, dz, way], recv_m.at[layer, dz, way],
                    ms_sem.at[layer, dz, way], mr_sem.at[layer, dz, way], device,
                )

        def stage_mine(dz):
            halves = []
            for way, low in ((0, 0), (1, HALF)):
                await_into(recv_m.at[layer, dz, way], mr_sem.at[layer, dz, way])
                merged = recv_m[layer, dz, way].astype(jnp.float32)
                direct = recv_x[layer, dz, 1 - way, HALF:BLOCK].astype(jnp.float32)
                halves.append(own(dz, 0, low, HALF) + merged + direct)
            whole = jnp.concatenate(halves, axis=0)
            if dz == 0:
                return whole
            send_z[layer, dz - 1] = whole.astype(jnp.bfloat16)
            push(
                send_z.at[layer, dz - 1], recv_z.at[layer, dz - 1],
                zs_sem.at[layer, dz - 1], zr_sem.at[layer, dz - 1], peers[dz],
            )
            return None

        for dz in DZ_ORDER:
            stage_core(dz)
        summed = None
        for step in range(len(DZ_ORDER) + 2):
            if step < 4:
                stage_far(DZ_ORDER[step])
            if 1 <= step < 5:
                stage_near(DZ_ORDER[step - 1])
            if step >= 2:
                summed = stage_mine(DZ_ORDER[step - 2])
        for dz in DZ_ORDER[:3]:
            await_into(recv_z.at[layer, dz - 1], zr_sem.at[layer, dz - 1])
            summed = summed + recv_z[layer, dz - 1].astype(jnp.float32)
        hidden = jnp.dot(
            summed.astype(jnp.bfloat16), weight_v[layer], preferred_element_type=jnp.float32
        )
        if layer + 1 < LAYERS:
            helds[layer + 1][row] = jnp.maximum(hidden, 0.0).astype(jnp.bfloat16)
        else:
            out_ref[...] = hidden.astype(jnp.bfloat16)

    for copy in sent:
        copy.wait_send()


def shards(features, adjacency, block_rows, block_cols, counts, weights):
    bf16 = jnp.bfloat16
    out = pl.pallas_call(
        kernel,
        out_shape=jax.ShapeDtypeStruct((BLOCK, BLOCK), bf16),
        in_specs=[pl.BlockSpec(memory_space=pltpu.HBM)] * 6,
        out_specs=pl.BlockSpec(memory_space=pltpu.VMEM),
        scratch_shapes=[
            pltpu.VMEM((BLOCK, BLOCK, BLOCK), bf16),
            pltpu.VMEM((1, BLOCK), jnp.int32),
            pltpu.VMEM((1, BLOCK), jnp.int32),
            pltpu.VMEM((1, 1), jnp.int32),
            pltpu.VMEM((LAYERS, BLOCK, BLOCK), bf16),
            pltpu.VMEM((ROWS + 1, BLOCK, BLOCK), bf16),
            pltpu.VMEM((ROWS + 1, BLOCK, BLOCK), bf16),
            pltpu.VMEM((PAIRS + 1, BLOCK, BLOCK), jnp.float32),
            pltpu.VMEM((8, BLOCK), jnp.int32),
            pltpu.SMEM((8, BLOCK), jnp.int32),
            pltpu.VMEM((LAYERS, 4, 4, BLOCK, BLOCK), bf16),
            pltpu.VMEM((LAYERS, 4, 4, BLOCK, BLOCK), bf16),
            pltpu.VMEM((LAYERS, 4, 2, BLOCK, BLOCK), bf16),
            pltpu.VMEM((LAYERS, 4, 2, BLOCK, BLOCK), bf16),
            pltpu.VMEM((LAYERS, 4, 2, HALF, BLOCK), bf16),
            pltpu.VMEM((LAYERS, 4, 2, HALF, BLOCK), bf16),
            pltpu.VMEM((LAYERS, 3, BLOCK, BLOCK), bf16),
            pltpu.VMEM((LAYERS, 3, BLOCK, BLOCK), bf16),
            pltpu.SemaphoreType.DMA((7,)),
            pltpu.SemaphoreType.DMA((LAYERS, 30)),
            pltpu.SemaphoreType.DMA((LAYERS, 2 * ROWS)),
            pltpu.SemaphoreType.DMA((LAYERS, 4)),
            pltpu.SemaphoreType.DMA((LAYERS, 4)),
            pltpu.SemaphoreType.DMA((LAYERS, 4, 2)),
            pltpu.SemaphoreType.DMA((LAYERS, 4, 2)),
            pltpu.SemaphoreType.DMA((LAYERS, 4, 2)),
            pltpu.SemaphoreType.DMA((LAYERS, 4, 2)),
            pltpu.SemaphoreType.DMA((LAYERS, 3)),
            pltpu.SemaphoreType.DMA((LAYERS, 3)),
        ],
        compiler_params=pltpu.CompilerParams(
            collective_id=0, has_side_effects=True, vmem_limit_bytes=63 * 1024 * 1024
        ),
        cost_estimate=pl.CostEstimate(
            flops=2 * LAYERS * 2 * BLOCK**4, bytes_accessed=2 * BLOCK**3, transcendentals=0
        ),
    )(features[0, 0], adjacency[0, 0], block_rows[0], block_cols[0], counts, weights)
    return out[None, None]


def solution(mesh):
    placed = (
        P("row", "col", None, None),
        P("row", "col", None, None, None),
        P("row", "col", None),
        P("row", "col", None),
        P("row", "col"),
        P(),
    )
    return jax.shard_map(
        shards, mesh=mesh, in_specs=placed, out_specs=P("row", "col", None, None), check_vma=False
    )
```

```python
import functools

import jax
import jax.numpy as jnp
from jax import lax
from jax.experimental import pallas as pl
from jax.experimental.pallas import tpu as pltpu
from jax.sharding import PartitionSpec as P

LAYERS = 2
BLOCK = 128
HALF = 64
ROWS = 16
PAIRS = 80
DZ_ORDER = (2, 1, 3, 0)
DX_ORDER = (2, 1, 3, 0)
CHUNKS = [(half, dz) for half in (0, 1) for dz in (2, 1, 3)] + [(0, 0), (1, 0)]
MESH = pl.DeviceIdType.MESH


def turned(vector):
    return jnp.transpose(jnp.broadcast_to(vector, (BLOCK, BLOCK)))


def slot_table(rows, cols, count):
    lane = lax.broadcasted_iota(jnp.int32, (BLOCK, BLOCK), 1)
    sub = lax.broadcasted_iota(jnp.int32, (BLOCK, BLOCK), 0)
    one = lane[:1]
    live = one < count
    rows = jnp.where(live, rows, BLOCK)
    rows_b = jnp.broadcast_to(rows, (BLOCK, BLOCK))
    rows_t = turned(rows)
    rank = jnp.sum(((rows_b == rows_t) & (sub < lane)).astype(jnp.int32), axis=0, keepdims=True)
    sizes = jnp.sum((rows_t == lane).astype(jnp.int32), axis=0, keepdims=True)
    pairs = turned((sizes + 1) >> 1)
    firsts = jnp.sum(jnp.where(sub < lane, pairs, 0), axis=0, keepdims=True)
    before = jnp.sum(jnp.where(sub < rows_b, pairs, 0), axis=0, keepdims=True)
    place = jnp.where(live, 2 * before + rank, 4 * BLOCK)
    packed = turned(place * 4096 + cols * BLOCK + one)
    place_t = packed >> 12
    value = (packed & 4095) - ROWS * BLOCK
    tables = [
        jnp.sum(jnp.where(place_t == lane + base, value, 0), axis=0, keepdims=True) + ROWS * BLOCK
        for base in (0, BLOCK)
    ]
    return firsts, tables[0], tables[1]


def kernel(
    feat_hbm, adj_hbm, rows_hbm, cols_hbm, count_hbm, weight_hbm, out_ref,
    adj, rows_v, cols_v, count_v, weight_v, held_0, held_1, prefix, table_v, table_s,
    send_c, recv_c, send_x, recv_x, send_z, recv_z,
    local_sem, gs_sem, gr_sem, cs_sem, cr_sem, xs_sem, xr_sem, zs_sem, zr_sem,
):
    row, col = lax.axis_index("row"), lax.axis_index("col")
    zh, y = row // 4, row % 4
    zl, x, core = col // 8, (col // 2) % 4, col % 2

    def at_row(dz, dy):
        return ((zh + dz) % 4) * 4 + (y + dy) % 4

    def at_col(dz, dx, other):
        side = 1 - core if other else core
        return ((zl + dz) % 4) * 8 + ((x + dx) % 4) * 2 + side

    z_up, z_down = (at_row(1, 0), col), (at_row(3, 0), col)
    z_across = (at_row(2, 0), col)
    y_peers = {dy: (at_row(0, dy), col) for dy in (1, 2, 3)}
    sibling = (row, at_col(0, 0, True))
    peers = {
        (dz, dx): (row, at_col(dz, dx, False))
        for dz in range(4) for dx in range(4) if (dz, dx) != (0, 0)
    }

    helds = (held_0, held_1)
    loads = [
        pltpu.make_async_copy(source, target, local_sem.at[at])
        for at, (source, target) in enumerate((
            (rows_hbm, rows_v), (cols_hbm, cols_v), (count_hbm, count_v),
            (feat_hbm, held_0.at[row]), (weight_hbm, weight_v), (adj_hbm, adj),
        ))
    ]
    barrier = pltpu.get_barrier_semaphore()
    partners = [z_up, z_down, *y_peers.values(), *peers.values(), sibling]
    for partner in partners:
        pl.semaphore_signal(barrier, inc=1, device_id=partner, device_id_type=MESH)
    for load in loads:
        load.start()
    for held in helds:
        held[ROWS] = jnp.zeros((BLOCK, BLOCK), jnp.bfloat16)
    prefix[0] = jnp.zeros((BLOCK, BLOCK), jnp.float32)
    pl.semaphore_wait(barrier, len(partners))

    sent = []

    def push(src, dst, send_sem, recv_sem, device):
        copy = pltpu.make_async_remote_copy(
            src_ref=src, dst_ref=dst, send_sem=send_sem, recv_sem=recv_sem,
            device_id=device, device_id_type=MESH,
        )
        copy.start()
        sent.append(copy)

    def await_into(dst, recv_sem):
        pltpu.make_async_remote_copy(
            src_ref=dst, dst_ref=dst, send_sem=recv_sem, recv_sem=recv_sem,
            device_id=sibling, device_id_type=MESH,
        ).wait_recv()

    to_scalar = pltpu.make_async_copy(table_v, table_s, local_sem.at[6])

    def sort_slots():
        for load in loads[:3]:
            load.wait()
        firsts, low, high = slot_table(rows_v[...], cols_v[...], count_v[...])
        table_v[0:1] = firsts
        table_v[1:2] = low
        table_v[2:3] = high
        to_scalar.start()

    given = [0] * LAYERS

    def half_of(layer, origin, half):
        return helds[layer].at[origin, pl.ds(half * HALF, HALF)]

    def give(layer, dz, dy, half, device):
        origin = at_row(dz, dy)
        source = half_of(layer, origin, half)
        if layer == 0 and dz == 0 and dy == 0:
            source = feat_hbm.at[pl.ds(half * HALF, HALF)]
        push(
            source, half_of(layer, origin, half),
            gs_sem.at[layer, given[layer]], gr_sem.at[layer, 2 * origin + half], device,
        )
        given[layer] += 1

    def take(layer, dz, dy, half):
        origin = at_row(dz, dy)
        await_into(half_of(layer, origin, half), gr_sem.at[layer, 2 * origin + half])

    def spread(layer, dz, half):
        for dy in (2, 1, 3):
            give(layer, dz, 0, half, y_peers[dy])

    def gather_give(layer, half):
        if layer > 0:
            give(layer, 0, 0, half, z_across)
        ahead, behind = (z_up, z_down) if half == 0 else (z_down, z_up)
        give(layer, 0, 0, half, ahead)
        give(layer, 0, 0, half, behind)
        spread(layer, 0, half)

    def gather_take(layer):
        take(layer, 3, 0, 0)
        if layer == 0:
            give(layer, 3, 0, 0, z_up)
        spread(layer, 3, 0)
        take(layer, 1, 0, 1)
        if layer == 0:
            give(layer, 1, 0, 1, z_down)
        spread(layer, 1, 1)
        take(layer, 1, 0, 0)
        spread(layer, 1, 0)
        take(layer, 3, 0, 1)
        spread(layer, 3, 1)
        for half in (0, 1):
            take(layer, 2, 0, half)
            spread(layer, 2, half)
        for dz in (0, 3, 1, 2):
            for dy in (1, 3, 2):
                for half in (0, 1):
                    take(layer, dz, dy, half)

    def multiply(layer):
        held = helds[layer]
        total = jnp.zeros((BLOCK, BLOCK), jnp.float32)
        for pair in range(PAIRS):
            line, at = 1 + pair // HALF, 2 * pair % BLOCK
            first, second = table_s[line, at], table_s[line, at + 1]
            left = jnp.concatenate([adj[first & 127], adj[second & 127]], axis=1)
            right = jnp.concatenate([held[first >> 7], held[second >> 7]], axis=0)
            total = total + jnp.dot(left, right, preferred_element_type=jnp.float32)
            prefix[pair + 1] = total

    def partial(half, dz, dx, other):
        index = at_col(dz, dx, other)
        span = pl.ds(half * HALF, HALF)
        return prefix[table_s[0, index + 1], span] - prefix[table_s[0, index], span]

    def own(layer, half, dz, dx):
        from_sibling = recv_c[layer, half, dz, dx].astype(jnp.float32)
        return partial(half, dz, dx, False) + from_sibling

    def stage_core(layer, half, dz):
        for dx in DX_ORDER:
            send_c[layer, half, dz, dx] = partial(half, dz, dx, True).astype(jnp.bfloat16)
        at = (layer, half, dz)
        push(send_c.at[at], recv_c.at[at], cs_sem.at[at], cr_sem.at[at], sibling)

    def stage_far(layer, half, dz):
        at = (layer, half, dz)
        await_into(recv_c.at[at], cr_sem.at[at])
        for dx in DX_ORDER:
            if dx == 0 and (half == 0 or dz == 0):
                continue
            at = (layer, half, dz, dx)
            send_x[at] = own(layer, half, dz, dx).astype(jnp.bfloat16)
            device = peers[dz if half == 1 else 0, dx]
            push(send_x.at[at], recv_x.at[at], xs_sem.at[at], xr_sem.at[at], device)

    def collect(layer, half, dz, dx, whole):
        at = (layer, half, dz, dx)
        await_into(recv_x.at[at], xr_sem.at[at])
        return whole + recv_x[at].astype(jnp.float32)

    def stage_mine(layer, dz):
        whole = own(layer, 0, dz, 0)
        for dx in (1, 3, 2):
            whole = collect(layer, 0, dz, dx, whole)
        if dz > 0:
            at = (layer, dz - 1)
            send_z[at] = whole.astype(jnp.bfloat16)
            push(send_z.at[at], recv_z.at[at], zs_sem.at[at], zr_sem.at[at], peers[dz, 0])
        return whole

    def finish(layer, half, whole):
        hidden = jnp.dot(
            whole.astype(jnp.bfloat16), weight_v[layer], preferred_element_type=jnp.float32
        )
        span = pl.ds(half * HALF, HALF)
        if layer + 1 < LAYERS:
            helds[layer + 1][row, span] = jnp.maximum(hidden, 0.0).astype(jnp.bfloat16)
            gather_give(layer + 1, half)
        else:
            out_ref[span] = hidden.astype(jnp.bfloat16)

    for half in (0, 1):
        gather_give(0, half)
    sort_slots()
    for layer in range(LAYERS):
        gather_take(layer)
        if layer == 0:
            to_scalar.wait()
            for load in loads[3:]:
                load.wait()
        multiply(layer)
        for half, dz in CHUNKS:
            stage_core(layer, half, dz)
        for half, dz in CHUNKS:
            stage_far(layer, half, dz)
        for dz in DZ_ORDER:
            upper = stage_mine(layer, dz)
        for dz in DZ_ORDER[:3]:
            at = (layer, dz - 1)
            await_into(recv_z.at[at], zr_sem.at[at])
            upper = upper + recv_z[at].astype(jnp.float32)
        finish(layer, 0, upper)
        lower = own(layer, 1, 0, 0)
        for dz in DZ_ORDER:
            for dx in (1, 3, 2, 0):
                if (dz, dx) != (0, 0):
                    lower = collect(layer, 1, dz, dx, lower)
        finish(layer, 1, lower)

    for copy in sent:
        copy.wait_send()


def shards(features, adjacency, block_rows, block_cols, counts, weights):
    bf16 = jnp.bfloat16
    out = pl.pallas_call(
        kernel,
        out_shape=jax.ShapeDtypeStruct((BLOCK, BLOCK), bf16),
        in_specs=[pl.BlockSpec(memory_space=pltpu.HBM)] * 6,
        out_specs=pl.BlockSpec(memory_space=pltpu.VMEM),
        scratch_shapes=[
            pltpu.VMEM((BLOCK, BLOCK, BLOCK), bf16),
            pltpu.VMEM((1, BLOCK), jnp.int32),
            pltpu.VMEM((1, BLOCK), jnp.int32),
            pltpu.VMEM((1, 1), jnp.int32),
            pltpu.VMEM((LAYERS, BLOCK, BLOCK), bf16),
            pltpu.VMEM((ROWS + 1, BLOCK, BLOCK), bf16),
            pltpu.VMEM((ROWS + 1, BLOCK, BLOCK), bf16),
            pltpu.VMEM((PAIRS + 1, BLOCK, BLOCK), jnp.float32),
            pltpu.VMEM((8, BLOCK), jnp.int32),
            pltpu.SMEM((8, BLOCK), jnp.int32),
            pltpu.VMEM((LAYERS, 2, 4, 4, HALF, BLOCK), bf16),
            pltpu.VMEM((LAYERS, 2, 4, 4, HALF, BLOCK), bf16),
            pltpu.VMEM((LAYERS, 2, 4, 4, HALF, BLOCK), bf16),
            pltpu.VMEM((LAYERS, 2, 4, 4, HALF, BLOCK), bf16),
            pltpu.VMEM((LAYERS, 3, HALF, BLOCK), bf16),
            pltpu.VMEM((LAYERS, 3, HALF, BLOCK), bf16),
            pltpu.SemaphoreType.DMA((7,)),
            pltpu.SemaphoreType.DMA((LAYERS, 34)),
            pltpu.SemaphoreType.DMA((LAYERS, 2 * ROWS)),
            pltpu.SemaphoreType.DMA((LAYERS, 2, 4)),
            pltpu.SemaphoreType.DMA((LAYERS, 2, 4)),
            pltpu.SemaphoreType.DMA((LAYERS, 2, 4, 4)),
            pltpu.SemaphoreType.DMA((LAYERS, 2, 4, 4)),
            pltpu.SemaphoreType.DMA((LAYERS, 3)),
            pltpu.SemaphoreType.DMA((LAYERS, 3)),
        ],
        compiler_params=pltpu.CompilerParams(
            collective_id=0, has_side_effects=True, vmem_limit_bytes=63 * 1024 * 1024
        ),
        cost_estimate=pl.CostEstimate(
            flops=2 * LAYERS * 2 * BLOCK**4, bytes_accessed=2 * BLOCK**3, transcendentals=0
        ),
    )(features[0, 0], adjacency[0, 0], block_rows[0], block_cols[0], counts, weights)
    return out[None, None]


def solution(mesh):
    placed = (
        P("row", "col", None, None),
        P("row", "col", None, None, None),
        P("row", "col", None),
        P("row", "col", None),
        P("row", "col"),
        P(),
    )
    return jax.shard_map(
        shards, mesh=mesh, in_specs=placed, out_specs=P("row", "col", None, None), check_vma=False
    )
```

```python
import functools

import jax
import jax.numpy as jnp
from jax import lax
from jax.experimental import pallas as pl
from jax.experimental.pallas import tpu as pltpu
from jax.sharding import PartitionSpec as P

LAYERS = 2
BLOCK = 128
HALF = 64
ROWS = 16
SLOTS = 128
COLS = 32
DZ_ORDER = (2, 1, 3, 0)
DX_ORDER = (2, 1, 3, 0)
CHUNKS = [(half, dz) for half in (0, 1) for dz in (2, 1, 3)] + [(0, 0), (1, 0)]
Y_WAIT = (0, 1, 2, 1)
LAST = [((2, 0), (2, 1)), ((2, 2), (2, 3))]
MESH = pl.DeviceIdType.MESH


def turned(vector):
    return jnp.transpose(jnp.broadcast_to(vector, (BLOCK, BLOCK)))


def slot_table(rows, cols, count):
    lane = lax.broadcasted_iota(jnp.int32, (BLOCK, BLOCK), 1)
    sub = lax.broadcasted_iota(jnp.int32, (BLOCK, BLOCK), 0)
    keys = jnp.where(lane[:1] < count, rows * ROWS + cols, 4 * BLOCK)
    keys_t = turned(keys)

    def last(found):
        slot = jnp.max(jnp.where(found, sub, -1), axis=0, keepdims=True)
        return jnp.where(slot < 0, SLOTS, slot)

    lines = [last(keys_t == lane + line * BLOCK) for line in range(4)]
    return lines + [last((keys_t == keys) & (sub < lane))]


def kernel(
    feat_hbm, adj_hbm, rows_hbm, cols_hbm, count_hbm, weight_hbm, out_ref,
    adj, rows_v, cols_v, count_v, weight_v, held_0, held_1, sums, merged, totals, table_v, table_s,
    send_c, recv_c, send_a, recv_a, send_b, recv_b, send_z, recv_z,
    local_sem, sent_sem, gz_sem, gy_sem, cr_sem, ar_sem, br_sem, zr_sem,
):
    row, col = lax.axis_index("row"), lax.axis_index("col")
    zh, y = row // 4, row % 4
    zl, x, core = col // 8, (col // 2) % 4, col % 2

    def at_row(dz, dy):
        return ((zh + dz) % 4) * 4 + (y + dy) % 4

    def at_col(dz, dx, other):
        side = 1 - core if other else core
        return ((zl + dz) % 4) * 8 + ((x + dx) % 4) * 2 + side

    z_up, z_down = (at_row(1, 0), col), (at_row(3, 0), col)
    y_peers = {dy: (at_row(0, dy), col) for dy in (1, 2, 3)}
    sibling = (row, at_col(0, 0, True))
    peers = {
        (dz, dx): (row, at_col(dz, dx, False))
        for dz in range(4) for dx in range(4) if (dz, dx) != (0, 0)
    }

    helds = (held_0, held_1)
    loads = [
        pltpu.make_async_copy(source, target, local_sem.at[at])
        for at, (source, target) in enumerate((
            (rows_hbm, rows_v), (cols_hbm, cols_v), (count_hbm, count_v),
            (feat_hbm, held_0.at[row]), (weight_hbm, weight_v), (adj_hbm, adj),
        ))
    ]
    barrier = pltpu.get_barrier_semaphore()
    partners = [z_up, z_down, *y_peers.values(), *peers.values(), sibling]
    for partner in partners:
        pl.semaphore_signal(barrier, inc=1, device_id=partner, device_id_type=MESH)
    for load in loads:
        load.start()
    sums[SLOTS] = jnp.zeros((BLOCK, BLOCK), jnp.float32)
    merged[SLOTS] = jnp.zeros((BLOCK, BLOCK), jnp.bfloat16)
    pl.semaphore_wait(barrier, len(partners))

    def push(src, dst, send_sem, recv_sem, device):
        pltpu.make_async_remote_copy(
            src_ref=src, dst_ref=dst, send_sem=send_sem, recv_sem=recv_sem,
            device_id=device, device_id_type=MESH,
        ).start()

    def await_into(dst, recv_sem):
        pltpu.make_async_remote_copy(
            src_ref=dst, dst_ref=dst, send_sem=recv_sem, recv_sem=recv_sem,
            device_id=sibling, device_id_type=MESH,
        ).wait_recv()

    to_scalar = pltpu.make_async_copy(table_v, table_s, local_sem.at[6])

    def sort_slots():
        for load in loads[:3]:
            load.wait()
        for line, row_of in enumerate(slot_table(rows_v[...], cols_v[...], count_v[...])):
            table_v[line : line + 1] = row_of
        to_scalar.start()
        to_scalar.wait()
        for load in loads[3:]:
            load.wait()

        def add_slots(step, carry):
            for part in range(8):
                slot = step * 8 + part
                total = adj[slot].astype(jnp.float32) + sums[table_s[4, slot]]
                sums[slot] = total
                merged[slot] = total.astype(jnp.bfloat16)
            return carry

        lax.fori_loop(0, SLOTS // 8, add_slots, 0)

    def half_of(layer, origin, half):
        return helds[layer].at[origin, pl.ds(half * HALF, HALF)]

    def give(layer, dz, half, recv_sem, device):
        origin = at_row(dz, 0)
        target = half_of(layer, origin, half)
        source = target
        if layer == 0 and dz == 0:
            source = feat_hbm.at[pl.ds(half * HALF, HALF)]
        push(source, target, sent_sem.at[layer, 0], recv_sem, device)

    def give_z(layer, dz, half, step):
        away = (dz - step) % 4
        device = (at_row(step, 0), col)
        give(layer, dz, half, gz_sem.at[layer, 2 * (away - 1) + half], device)

    def take_z(layer, dz, half):
        await_into(half_of(layer, at_row(dz, 0), half), gz_sem.at[layer, 2 * (dz - 1) + half])

    def spread(layer, dz, half):
        for dy in (2, 1, 3):
            give(layer, dz, half, gy_sem.at[layer, Y_WAIT[dz]], y_peers[dy])

    def take_y(layer, wait, blocks):
        await_into(helds[layer].at[pl.ds(0, blocks)], gy_sem.at[layer, wait])

    def gather_give(layer, half):
        if layer > 0:
            give_z(layer, 0, half, 2)
        ahead = 1 if half == 0 else 3
        give_z(layer, 0, half, ahead)
        give_z(layer, 0, half, 4 - ahead)
        spread(layer, 0, half)

    def gather_take(layer):
        for dz, half, step in ((3, 0, 1), (1, 1, 3), (1, 0, 0), (3, 1, 0)):
            take_z(layer, dz, half)
            if layer == 0 and step > 0:
                give_z(layer, dz, half, step)
            spread(layer, dz, half)
        take_y(layer, 0, 3)
        multiply(layer, [((0, 0), (0, 1)), ((0, 2), (0, 3))], True)
        for half in (0, 1):
            take_z(layer, 2, half)
            spread(layer, 2, half)
        multiply(layer, [((3, 0), (1, 0))], False)
        take_y(layer, 1, 6)
        multiply(layer, [((3, 1), (3, 3)), ((1, 1), (1, 3))], False)
        multiply(layer, [((3, 2), (1, 2))], False)
        take_y(layer, 2, 3)

    def products(layer, groups, block):
        held = helds[layer]
        total = None
        for group in groups:
            origins = [at_row(*step) for step in group]
            slots = [table_s[block // 8, block % 8 * ROWS + origin] for origin in origins]
            left = jnp.concatenate([merged[slot] for slot in slots], axis=1)
            right = jnp.concatenate([held[origin] for origin in origins], axis=0)
            term = jnp.dot(left, right, preferred_element_type=jnp.float32)
            total = term if total is None else total + term
        return total

    def multiply(layer, groups, fresh):
        def step(at, carry):
            for inner in range(16):
                block = at * 16 + inner
                total = products(layer, groups, block)
                totals[block] = total if fresh else totals[block] + total
            return carry

        lax.fori_loop(0, COLS // 16, step, 0)

    def complete(layer, dz, dx, other):
        block = at_col(dz, dx, other)
        return totals[block] + products(layer, LAST, block)

    def own(layer, half, dz, dx):
        from_sibling = recv_c[layer, dz, half, dx].astype(jnp.float32)
        return totals[at_col(dz, dx, False), pl.ds(half * HALF, HALF)] + from_sibling

    def stage_core(layer, dz):
        for dx in DX_ORDER:
            whole = complete(layer, dz, dx, True).astype(jnp.bfloat16)
            send_c[layer, dz, 0, dx] = whole[:HALF]
            send_c[layer, dz, 1, dx] = whole[HALF:]
        at = (layer, dz)
        push(send_c.at[at], recv_c.at[at], sent_sem.at[layer, 1], cr_sem.at[at], sibling)

    def stage_far(layer, half, dz):
        if half == 0:
            await_into(recv_c.at[layer, dz], cr_sem.at[layer, dz])
        for dx in DX_ORDER:
            if half == 0 and dx > 0:
                at = (layer, dz, dx - 1)
                send_a[at] = own(layer, 0, dz, dx).astype(jnp.bfloat16)
                push(
                    send_a.at[at], recv_a.at[at],
                    sent_sem.at[layer, 2], ar_sem.at[layer, dz], peers[0, dx],
                )
            if half == 1 and (dz, dx) != (0, 0):
                at = (layer, 4 * dz + dx - 1)
                send_b[at] = own(layer, 1, dz, dx).astype(jnp.bfloat16)
                push(
                    send_b.at[at], recv_b.at[at],
                    sent_sem.at[layer, 3], br_sem.at[layer], peers[dz, dx],
                )

    def stage_mine(layer, dz):
        await_into(recv_a.at[layer, dz], ar_sem.at[layer, dz])
        whole = own(layer, 0, dz, 0)
        for at in range(3):
            whole = whole + recv_a[layer, dz, at].astype(jnp.float32)
        if dz > 0:
            at = (layer, dz - 1)
            send_z[at] = whole.astype(jnp.bfloat16)
            push(send_z.at[at], recv_z.at[at], sent_sem.at[layer, 4], zr_sem.at[layer], peers[dz, 0])
        return whole

    def finish(layer, half, whole):
        hidden = jnp.dot(
            whole.astype(jnp.bfloat16), weight_v[layer], preferred_element_type=jnp.float32
        )
        span = pl.ds(half * HALF, HALF)
        if layer + 1 < LAYERS:
            helds[layer + 1][row, span] = jnp.maximum(hidden, 0.0).astype(jnp.bfloat16)
            gather_give(layer + 1, half)
        else:
            out_ref[span] = hidden.astype(jnp.bfloat16)

    for half in (0, 1):
        gather_give(0, half)
    sort_slots()
    for layer in range(LAYERS):
        gather_take(layer)
        for dz in DZ_ORDER:
            stage_core(layer, dz)
        for dz in DZ_ORDER:
            for dx in DX_ORDER:
                totals[at_col(dz, dx, False)] = complete(layer, dz, dx, False)
        for half, dz in CHUNKS:
            stage_far(layer, half, dz)
        for dz in DZ_ORDER:
            upper = stage_mine(layer, dz)
        await_into(recv_z.at[layer], zr_sem.at[layer])
        for at in range(3):
            upper = upper + recv_z[layer, at].astype(jnp.float32)
        finish(layer, 0, upper)
        await_into(recv_b.at[layer], br_sem.at[layer])
        lower = own(layer, 1, 0, 0)
        for at in range(15):
            lower = lower + recv_b[layer, at].astype(jnp.float32)
        finish(layer, 1, lower)

    for layer in range(LAYERS):
        sources = (
            helds[layer].at[pl.ds(0, 15)], send_c.at[layer], send_a.at[layer],
            send_b.at[layer], send_z.at[layer],
        )
        for kind, source in enumerate(sources):
            pltpu.make_async_remote_copy(
                src_ref=source, dst_ref=source,
                send_sem=sent_sem.at[layer, kind], recv_sem=sent_sem.at[layer, kind],
                device_id=sibling, device_id_type=MESH,
            ).wait_send()


def shards(features, adjacency, block_rows, block_cols, counts, weights):
    bf16 = jnp.bfloat16
    out = pl.pallas_call(
        kernel,
        out_shape=jax.ShapeDtypeStruct((BLOCK, BLOCK), bf16),
        in_specs=[pl.BlockSpec(memory_space=pltpu.HBM)] * 6,
        out_specs=pl.BlockSpec(memory_space=pltpu.VMEM),
        scratch_shapes=[
            pltpu.VMEM((BLOCK, BLOCK, BLOCK), bf16),
            pltpu.VMEM((1, BLOCK), jnp.int32),
            pltpu.VMEM((1, BLOCK), jnp.int32),
            pltpu.VMEM((1, 1), jnp.int32),
            pltpu.VMEM((LAYERS, BLOCK, BLOCK), bf16),
            pltpu.VMEM((ROWS, BLOCK, BLOCK), bf16),
            pltpu.VMEM((ROWS, BLOCK, BLOCK), bf16),
            pltpu.VMEM((SLOTS + 1, BLOCK, BLOCK), jnp.float32),
            pltpu.VMEM((SLOTS + 1, BLOCK, BLOCK), bf16),
            pltpu.VMEM((COLS, BLOCK, BLOCK), jnp.float32),
            pltpu.VMEM((8, BLOCK), jnp.int32),
            pltpu.SMEM((8, BLOCK), jnp.int32),
            pltpu.VMEM((LAYERS, 4, 2, 4, HALF, BLOCK), bf16),
            pltpu.VMEM((LAYERS, 4, 2, 4, HALF, BLOCK), bf16),
            pltpu.VMEM((LAYERS, 4, 3, HALF, BLOCK), bf16),
            pltpu.VMEM((LAYERS, 4, 3, HALF, BLOCK), bf16),
            pltpu.VMEM((LAYERS, 15, HALF, BLOCK), bf16),
            pltpu.VMEM((LAYERS, 15, HALF, BLOCK), bf16),
            pltpu.VMEM((LAYERS, 3, HALF, BLOCK), bf16),
            pltpu.VMEM((LAYERS, 3, HALF, BLOCK), bf16),
            pltpu.SemaphoreType.DMA((7,)),
            pltpu.SemaphoreType.DMA((LAYERS, 5)),
            pltpu.SemaphoreType.DMA((LAYERS, 6)),
            pltpu.SemaphoreType.DMA((LAYERS, 3)),
            pltpu.SemaphoreType.DMA((LAYERS, 4)),
            pltpu.SemaphoreType.DMA((LAYERS, 4)),
            pltpu.SemaphoreType.DMA((LAYERS,)),
            pltpu.SemaphoreType.DMA((LAYERS,)),
        ],
        compiler_params=pltpu.CompilerParams(
            collective_id=0, has_side_effects=True, vmem_limit_bytes=63 * 1024 * 1024
        ),
        cost_estimate=pl.CostEstimate(
            flops=2 * LAYERS * ROWS * COLS * BLOCK**3, bytes_accessed=2 * BLOCK**3, transcendentals=0
        ),
    )(features[0, 0], adjacency[0, 0], block_rows[0], block_cols[0], counts, weights)
    return out[None, None]


def solution(mesh):
    placed = (
        P("row", "col", None, None),
        P("row", "col", None, None, None),
        P("row", "col", None),
        P("row", "col", None),
        P("row", "col"),
        P(),
    )
    return jax.shard_map(
        shards, mesh=mesh, in_specs=placed, out_specs=P("row", "col", None, None), check_vma=False
    )
```

```python
import functools

import jax
import jax.numpy as jnp
from jax import lax
from jax.experimental import pallas as pl
from jax.experimental.pallas import tpu as pltpu
from jax.sharding import PartitionSpec as P

LAYERS = 2
BLOCK = 128
HALF = 64
ROWS = 16
SLOTS = 128
COLS = 32
DZ_ORDER = (2, 1, 3, 0)
DX_ORDER = (2, 1, 3, 0)
CHUNKS = [(0, 2), (1, 2), (0, 1), (0, 3), (1, 1), (1, 3), (0, 0), (1, 0)]
SUMMED = [(0, 2), (1, 2), (0, 1), (0, 3), (0, 0)]
DIRECT = [0, 1, 3]
HOLD = True
ACROSS_LAST = True
Y_WAIT = (0, 1, 2, 1)
LAST = [((2, 0), (2, 1)), ((2, 2), (2, 3))]
MESH = pl.DeviceIdType.MESH


def turned(vector):
    return jnp.transpose(jnp.broadcast_to(vector, (BLOCK, BLOCK)))


def slot_table(rows, cols, count):
    lane = lax.broadcasted_iota(jnp.int32, (BLOCK, BLOCK), 1)
    sub = lax.broadcasted_iota(jnp.int32, (BLOCK, BLOCK), 0)
    keys = jnp.where(lane[:1] < count, rows * ROWS + cols, 4 * BLOCK)
    keys_t = turned(keys)

    def last(found):
        slot = jnp.max(jnp.where(found, sub, -1), axis=0, keepdims=True)
        return jnp.where(slot < 0, SLOTS, slot)

    lines = [last(keys_t == lane + line * BLOCK) for line in range(4)]
    return lines + [last((keys_t == keys) & (sub < lane))]


def kernel(
    feat_hbm, adj_hbm, rows_hbm, cols_hbm, count_hbm, weight_hbm, out_ref,
    adj, rows_v, cols_v, count_v, weight_v, held_0, held_1, sums, merged, totals, table_v, table_s,
    send_c, recv_c, send_a, recv_a, send_b, recv_b, send_z, recv_z,
    local_sem, sent_sem, gz_sem, gy_sem, cr_sem, ar_sem, br_sem, zr_sem, entered_sem,
):
    row, col = lax.axis_index("row"), lax.axis_index("col")
    zh, y = row // 4, row % 4
    zl, x, core = col // 8, (col // 2) % 4, col % 2

    def at_row(dz, dy):
        return ((zh + dz) % 4) * 4 + (y + dy) % 4

    def at_col(dz, dx, other):
        side = 1 - core if other else core
        return ((zl + dz) % 4) * 8 + ((x + dx) % 4) * 2 + side

    z_up, z_down = (at_row(1, 0), col), (at_row(3, 0), col)
    y_peers = {dy: (at_row(0, dy), col) for dy in (1, 2, 3)}
    sibling = (row, at_col(0, 0, True))
    peers = {
        (dz, dx): (row, at_col(dz, dx, False))
        for dz in range(4) for dx in range(4) if (dz, dx) != (0, 0)
    }

    helds = (held_0, held_1)
    loads = [
        pltpu.make_async_copy(source, target, local_sem.at[at])
        for at, (source, target) in enumerate((
            (rows_hbm, rows_v), (cols_hbm, cols_v), (count_hbm, count_v),
            (feat_hbm, held_0.at[row]), (weight_hbm, weight_v), (adj_hbm, adj),
        ))
    ]
    barrier = pltpu.get_barrier_semaphore()
    near = [peers[0, 1], peers[0, 3], peers[1, 0], peers[3, 0]]
    partners = [z_up, z_down, *near, *y_peers.values(), sibling]
    for partner in partners:
        pl.semaphore_signal(barrier, inc=1, device_id=partner, device_id_type=MESH)
    for load in loads:
        load.start()
    sums[SLOTS] = jnp.zeros((BLOCK, BLOCK), jnp.float32)
    merged[SLOTS] = jnp.zeros((BLOCK, BLOCK), jnp.bfloat16)
    pl.semaphore_wait(barrier, len(partners))

    def push(src, dst, send_sem, recv_sem, device):
        pltpu.make_async_remote_copy(
            src_ref=src, dst_ref=dst, send_sem=send_sem, recv_sem=recv_sem,
            device_id=device, device_id_type=MESH,
        ).start()

    def tell_near(turn):
        for device in near:
            pl.semaphore_signal(entered_sem.at[turn], inc=1, device_id=device, device_id_type=MESH)

    def hear_near(turn):
        pl.semaphore_wait(entered_sem.at[turn], len(near))

    def await_into(dst, recv_sem):
        pltpu.make_async_remote_copy(
            src_ref=dst, dst_ref=dst, send_sem=recv_sem, recv_sem=recv_sem,
            device_id=sibling, device_id_type=MESH,
        ).wait_recv()

    def await_sent(src, send_sem):
        pltpu.make_async_remote_copy(
            src_ref=src, dst_ref=src, send_sem=send_sem, recv_sem=send_sem,
            device_id=sibling, device_id_type=MESH,
        ).wait_send()

    to_scalar = pltpu.make_async_copy(table_v, table_s, local_sem.at[6])

    def sort_slots():
        for load in loads[:3]:
            load.wait()
        for line, row_of in enumerate(slot_table(rows_v[...], cols_v[...], count_v[...])):
            table_v[line : line + 1] = row_of
        to_scalar.start()
        to_scalar.wait()
        for load in loads[3:]:
            load.wait()

        def add_slots(step, carry):
            for part in range(8):
                slot = step * 8 + part
                total = adj[slot].astype(jnp.float32) + sums[table_s[4, slot]]
                sums[slot] = total
                merged[slot] = total.astype(jnp.bfloat16)
            return carry

        lax.fori_loop(0, SLOTS // 8, add_slots, 0)

    def half_of(layer, origin, half):
        return helds[layer].at[origin, pl.ds(half * HALF, HALF)]

    def give(layer, dz, half, recv_sem, device):
        origin = at_row(dz, 0)
        target = half_of(layer, origin, half)
        source = target
        if layer == 0 and dz == 0:
            source = feat_hbm.at[pl.ds(half * HALF, HALF)]
        push(source, target, sent_sem.at[layer, 0], recv_sem, device)

    def give_z(layer, dz, half, step):
        away = (dz - step) % 4
        device = (at_row(step, 0), col)
        give(layer, dz, half, gz_sem.at[layer, 2 * (away - 1) + half], device)

    def take_z(layer, dz, half):
        await_into(half_of(layer, at_row(dz, 0), half), gz_sem.at[layer, 2 * (dz - 1) + half])

    def spread(layer, dz, half):
        for dy in (2, 1, 3):
            give(layer, dz, half, gy_sem.at[layer, Y_WAIT[dz]], y_peers[dy])

    def take_y(layer, wait, blocks):
        await_into(helds[layer].at[pl.ds(0, blocks)], gy_sem.at[layer, wait])

    def gather_give(layer, half):
        if layer > 0 and not ACROSS_LAST:
            give_z(layer, 0, half, 2)
        ahead = 1 if half == 0 else 3
        give_z(layer, 0, half, ahead)
        give_z(layer, 0, half, 4 - ahead)
        spread(layer, 0, half)
        if layer > 0 and ACROSS_LAST and half == 1:
            give_z(layer, 0, 0, 2)
            give_z(layer, 0, 1, 2)

    def gather_take(layer):
        for dz, half, step in ((3, 0, 1), (1, 1, 3), (1, 0, 0), (3, 1, 0)):
            take_z(layer, dz, half)
            if layer == 0 and step > 0:
                give_z(layer, dz, half, step)
            spread(layer, dz, half)
        if layer == 0:
            hear_near(1)
            tell_near(2)
        take_y(layer, 0, 3)
        multiply(layer, [((0, 0), (0, 1)), ((0, 2), (0, 3))], True)
        for half in (0, 1):
            take_z(layer, 2, half)
            spread(layer, 2, half)
        multiply(layer, [((3, 0), (1, 0))], False)
        take_y(layer, 1, 6)
        multiply(layer, [((3, 1), (3, 3)), ((1, 1), (1, 3)), ((3, 2), (1, 2))], False)
        take_y(layer, 2, 3)

    def products(layer, groups, block):
        held = helds[layer]
        total = None
        for group in groups:
            origins = [at_row(*step) for step in group]
            slots = [table_s[block // 8, block % 8 * ROWS + origin] for origin in origins]
            left = jnp.concatenate([merged[slot] for slot in slots], axis=1)
            right = jnp.concatenate([held[origin] for origin in origins], axis=0)
            term = jnp.dot(left, right, preferred_element_type=jnp.float32)
            total = term if total is None else total + term
        return total

    def multiply(layer, groups, fresh):
        def step(at, carry):
            for inner in range(16):
                block = at * 16 + inner
                total = products(layer, groups, block)
                totals[block] = total if fresh else totals[block] + total
            return carry

        lax.fori_loop(0, COLS // 16, step, 0)

    def complete(layer, dz, dx, other):
        block = at_col(dz, dx, other)
        return totals[block] + products(layer, LAST, block)

    def own(layer, half, dz, dx):
        from_sibling = recv_c[layer, dz, half, dx].astype(jnp.float32)
        return totals[at_col(dz, dx, False), pl.ds(half * HALF, HALF)] + from_sibling

    def stage_core(layer, dz):
        for dx in DX_ORDER:
            whole = complete(layer, dz, dx, True).astype(jnp.bfloat16)
            send_c[layer, dz, 0, dx] = whole[:HALF]
            send_c[layer, dz, 1, dx] = whole[HALF:]
        at = (layer, dz)
        push(send_c.at[at], recv_c.at[at], sent_sem.at[layer, 1], cr_sem.at[at], sibling)

    def stage_far(layer, half, dz):
        for dx in DX_ORDER:
            if (half, dz) in SUMMED:
                if dx > 0:
                    at = (layer, SUMMED.index((half, dz)))
                    send_a[*at, dx - 1] = own(layer, half, dz, dx).astype(jnp.bfloat16)
                    push(
                        send_a.at[*at, dx - 1], recv_a.at[*at, dx - 1],
                        sent_sem.at[layer, 5 if at[1] < 2 else 2], ar_sem.at[at], peers[0, dx],
                    )
            elif (dz, dx) != (0, 0):
                at = (layer, 4 * DIRECT.index(dz) + dx - 1)
                send_b[at] = own(layer, 1, dz, dx).astype(jnp.bfloat16)
                push(
                    send_b.at[at], recv_b.at[at],
                    sent_sem.at[layer, 3], br_sem.at[layer], peers[dz, dx],
                )

    def stage_mine(layer, half, dz):
        at = (layer, SUMMED.index((half, dz)))
        await_into(recv_a.at[at], ar_sem.at[at])
        whole = own(layer, half, dz, 0)
        for dx in range(3):
            whole = whole + recv_a[*at, dx].astype(jnp.float32)
        if dz > 0:
            send_z[at] = whole.astype(jnp.bfloat16)
            push(send_z.at[at], recv_z.at[at], sent_sem.at[layer, 4], zr_sem.at[layer], peers[dz, 0])
        return whole

    def finish(layer, half, whole):
        hidden = jnp.dot(
            whole.astype(jnp.bfloat16), weight_v[layer], preferred_element_type=jnp.float32
        )
        span = pl.ds(half * HALF, HALF)
        if layer + 1 < LAYERS:
            helds[layer + 1][row, span] = jnp.maximum(hidden, 0.0).astype(jnp.bfloat16)
            gather_give(layer + 1, half)
        else:
            out_ref[span] = hidden.astype(jnp.bfloat16)

    for half in (0, 1):
        gather_give(0, half)
    tell_near(0)
    sort_slots()
    hear_near(0)
    tell_near(1)
    for layer in range(LAYERS):
        gather_take(layer)
        for dz in DZ_ORDER:
            stage_core(layer, dz)
        if layer == 0:
            hear_near(2)
        for half, dz in CHUNKS:
            if half == 0:
                for dx in DX_ORDER:
                    totals[at_col(dz, dx, False)] = complete(layer, dz, dx, False)
                await_into(recv_c.at[layer, dz], cr_sem.at[layer, dz])
            if HOLD and (half, dz) == (1, 1):
                await_sent(send_a.at[layer, pl.ds(0, 2)], sent_sem.at[layer, 5])
            stage_far(layer, half, dz)
        for half, dz in SUMMED:
            upper = stage_mine(layer, half, dz)
        await_into(recv_z.at[layer], zr_sem.at[layer])
        for at, (half, dz) in enumerate(SUMMED):
            if half == 0 and dz > 0:
                upper = upper + recv_z[layer, at].astype(jnp.float32)
        finish(layer, 0, upper)
        await_into(recv_b.at[layer], br_sem.at[layer])
        lower = own(layer, 1, 0, 0)
        for at in range(11):
            lower = lower + recv_b[layer, at].astype(jnp.float32)
        lower = lower + recv_z[layer, SUMMED.index((1, 2))].astype(jnp.float32)
        finish(layer, 1, lower)

    for layer in range(LAYERS):
        sources = [
            helds[layer].at[pl.ds(0, 15)], send_c.at[layer], send_a.at[layer, pl.ds(2, 3)],
            send_b.at[layer], send_z.at[layer],
        ]
        if not HOLD:
            sources.append(send_a.at[layer, pl.ds(0, 2)])
        for kind, source in enumerate(sources):
            await_sent(source, sent_sem.at[layer, kind])


def shards(features, adjacency, block_rows, block_cols, counts, weights):
    bf16 = jnp.bfloat16
    out = pl.pallas_call(
        kernel,
        out_shape=jax.ShapeDtypeStruct((BLOCK, BLOCK), bf16),
        in_specs=[pl.BlockSpec(memory_space=pltpu.HBM)] * 6,
        out_specs=pl.BlockSpec(memory_space=pltpu.VMEM),
        scratch_shapes=[
            pltpu.VMEM((BLOCK, BLOCK, BLOCK), bf16),
            pltpu.VMEM((1, BLOCK), jnp.int32),
            pltpu.VMEM((1, BLOCK), jnp.int32),
            pltpu.VMEM((1, 1), jnp.int32),
            pltpu.VMEM((LAYERS, BLOCK, BLOCK), bf16),
            pltpu.VMEM((ROWS, BLOCK, BLOCK), bf16),
            pltpu.VMEM((ROWS, BLOCK, BLOCK), bf16),
            pltpu.VMEM((SLOTS + 1, BLOCK, BLOCK), jnp.float32),
            pltpu.VMEM((SLOTS + 1, BLOCK, BLOCK), bf16),
            pltpu.VMEM((COLS, BLOCK, BLOCK), jnp.float32),
            pltpu.VMEM((8, BLOCK), jnp.int32),
            pltpu.SMEM((8, BLOCK), jnp.int32),
            pltpu.VMEM((LAYERS, 4, 2, 4, HALF, BLOCK), bf16),
            pltpu.VMEM((LAYERS, 4, 2, 4, HALF, BLOCK), bf16),
            pltpu.VMEM((LAYERS, 5, 3, HALF, BLOCK), bf16),
            pltpu.VMEM((LAYERS, 5, 3, HALF, BLOCK), bf16),
            pltpu.VMEM((LAYERS, 11, HALF, BLOCK), bf16),
            pltpu.VMEM((LAYERS, 11, HALF, BLOCK), bf16),
            pltpu.VMEM((LAYERS, 4, HALF, BLOCK), bf16),
            pltpu.VMEM((LAYERS, 4, HALF, BLOCK), bf16),
            pltpu.SemaphoreType.DMA((7,)),
            pltpu.SemaphoreType.DMA((LAYERS, 6)),
            pltpu.SemaphoreType.DMA((LAYERS, 6)),
            pltpu.SemaphoreType.DMA((LAYERS, 3)),
            pltpu.SemaphoreType.DMA((LAYERS, 4)),
            pltpu.SemaphoreType.DMA((LAYERS, 5)),
            pltpu.SemaphoreType.DMA((LAYERS,)),
            pltpu.SemaphoreType.DMA((LAYERS,)),
            pltpu.SemaphoreType.REGULAR((3,)),
        ],
        compiler_params=pltpu.CompilerParams(
            collective_id=0, has_side_effects=True, vmem_limit_bytes=63 * 1024 * 1024
        ),
        cost_estimate=pl.CostEstimate(
            flops=2 * LAYERS * ROWS * COLS * BLOCK**3, bytes_accessed=2 * BLOCK**3, transcendentals=0
        ),
    )(features[0, 0], adjacency[0, 0], block_rows[0], block_cols[0], counts, weights)
    return out[None, None]


def solution(mesh):
    placed = (
        P("row", "col", None, None),
        P("row", "col", None, None, None),
        P("row", "col", None),
        P("row", "col", None),
        P("row", "col"),
        P(),
    )
    return jax.shard_map(
        shards, mesh=mesh, in_specs=placed, out_specs=P("row", "col", None, None), check_vma=False
    )
```

```python
import functools

import jax
import jax.numpy as jnp
from jax import lax
from jax.experimental import pallas as pl
from jax.experimental.pallas import tpu as pltpu
from jax.sharding import PartitionSpec as P

LAYERS = 2
BLOCK = 128
HALF = 64
ROWS = 16
SLOTS = 128
COLS = 32
DZ_ORDER = (2, 1, 3, 0)
DX_ORDER = (2, 1, 3, 0)
CHUNKS = [(0, 2), (1, 2), (0, 1), (0, 3), (1, 1), (1, 3), (0, 0), (1, 0)]
SUMMED = [(0, 2), (1, 2), (0, 1), (0, 3), (0, 0)]
DIRECT = [0, 1, 3]
Y_WAIT = (0, 1, 2, 1)
LAST = [((2, 0), (2, 1)), ((2, 2), (2, 3))]
MESH = pl.DeviceIdType.MESH


def turned(vector):
    return jnp.transpose(jnp.broadcast_to(vector, (BLOCK, BLOCK)))


def slot_table(rows, cols, count):
    lane = lax.broadcasted_iota(jnp.int32, (BLOCK, BLOCK), 1)
    sub = lax.broadcasted_iota(jnp.int32, (BLOCK, BLOCK), 0)
    keys = jnp.where(lane[:1] < count, rows * ROWS + cols, 4 * BLOCK)
    keys_t = turned(keys)

    def last(found):
        slot = jnp.max(jnp.where(found, sub, -1), axis=0, keepdims=True)
        return jnp.where(slot < 0, SLOTS, slot)

    lines = [last(keys_t == lane + line * BLOCK) for line in range(4)]
    return lines + [last((keys_t == keys) & (sub < lane))]


def kernel(
    feat_hbm, adj_hbm, rows_hbm, cols_hbm, count_hbm, weight_hbm, out_ref,
    adj, rows_v, cols_v, count_v, weight_v, held_0, held_1, sums, merged, totals, table_v, table_s,
    send_c, recv_c, send_a, recv_a, send_b, recv_b, send_z, recv_z,
    local_sem, sent_sem, gz_sem, gy_sem, cr_sem, ar_sem, br_sem, zr_sem, entered_sem,
):
    row, col = lax.axis_index("row"), lax.axis_index("col")
    zh, y = row // 4, row % 4
    zl, x, core = col // 8, (col // 2) % 4, col % 2

    def at_row(dz, dy):
        return ((zh + dz) % 4) * 4 + (y + dy) % 4

    def at_col(dz, dx, other):
        side = 1 - core if other else core
        return ((zl + dz) % 4) * 8 + ((x + dx) % 4) * 2 + side

    z_up, z_down = (at_row(1, 0), col), (at_row(3, 0), col)
    y_peers = {dy: (at_row(0, dy), col) for dy in (1, 2, 3)}
    sibling = (row, at_col(0, 0, True))
    peers = {
        (dz, dx): (row, at_col(dz, dx, False))
        for dz in range(4) for dx in range(4) if (dz, dx) != (0, 0)
    }

    helds = (held_0, held_1)
    loads = [
        pltpu.make_async_copy(source, target, local_sem.at[at])
        for at, (source, target) in enumerate((
            (rows_hbm, rows_v), (cols_hbm, cols_v), (count_hbm, count_v),
            (feat_hbm, held_0.at[row]), (weight_hbm, weight_v), (adj_hbm, adj),
        ))
    ]
    barrier = pltpu.get_barrier_semaphore()
    near = [peers[0, 1], peers[0, 3], peers[1, 0], peers[3, 0]]
    partners = [z_up, z_down, *near, *y_peers.values(), sibling]
    for partner in partners:
        pl.semaphore_signal(barrier, inc=1, device_id=partner, device_id_type=MESH)
    for load in loads:
        load.start()
    sums[SLOTS] = jnp.zeros((BLOCK, BLOCK), jnp.float32)
    merged[SLOTS] = jnp.zeros((BLOCK, BLOCK), jnp.bfloat16)
    pl.semaphore_wait(barrier, len(partners))

    def push(src, dst, send_sem, recv_sem, device):
        pltpu.make_async_remote_copy(
            src_ref=src, dst_ref=dst, send_sem=send_sem, recv_sem=recv_sem,
            device_id=device, device_id_type=MESH,
        ).start()

    def tell_near(turn):
        for device in near:
            pl.semaphore_signal(entered_sem.at[turn], inc=1, device_id=device, device_id_type=MESH)

    def hear_near(turn):
        pl.semaphore_wait(entered_sem.at[turn], len(near))

    def await_into(dst, recv_sem):
        pltpu.make_async_remote_copy(
            src_ref=dst, dst_ref=dst, send_sem=recv_sem, recv_sem=recv_sem,
            device_id=sibling, device_id_type=MESH,
        ).wait_recv()

    def await_sent(src, send_sem):
        pltpu.make_async_remote_copy(
            src_ref=src, dst_ref=src, send_sem=send_sem, recv_sem=send_sem,
            device_id=sibling, device_id_type=MESH,
        ).wait_send()

    def settle(layer, kinds):
        sources = (
            helds[layer].at[pl.ds(0, 15)], send_c.at[layer], send_a.at[layer, pl.ds(2, 3)],
            send_b.at[layer], send_z.at[layer],
        )
        for kind in kinds:
            await_sent(sources[kind], sent_sem.at[layer, kind])

    to_scalar = pltpu.make_async_copy(table_v, table_s, local_sem.at[6])

    def sort_slots():
        for load in loads[:3]:
            load.wait()
        for line, row_of in enumerate(slot_table(rows_v[...], cols_v[...], count_v[...])):
            table_v[line : line + 1] = row_of
        to_scalar.start()
        to_scalar.wait()
        for load in loads[3:]:
            load.wait()

        def add_slots(step, carry):
            for part in range(8):
                slot = step * 8 + part
                total = adj[slot].astype(jnp.float32) + sums[table_s[4, slot]]
                sums[slot] = total
                merged[slot] = total.astype(jnp.bfloat16)
            return carry

        lax.fori_loop(0, SLOTS // 8, add_slots, 0)

    def half_of(layer, origin, half):
        return helds[layer].at[origin, pl.ds(half * HALF, HALF)]

    def give(layer, dz, half, recv_sem, device):
        origin = at_row(dz, 0)
        target = half_of(layer, origin, half)
        source = target
        if layer == 0 and dz == 0:
            source = feat_hbm.at[pl.ds(half * HALF, HALF)]
        push(source, target, sent_sem.at[layer, 0], recv_sem, device)

    def give_z(layer, dz, half, step):
        away = (dz - step) % 4
        device = (at_row(step, 0), col)
        give(layer, dz, half, gz_sem.at[layer, 2 * (away - 1) + half], device)

    def take_z(layer, dz, half):
        await_into(half_of(layer, at_row(dz, 0), half), gz_sem.at[layer, 2 * (dz - 1) + half])

    def spread(layer, dz, half):
        for dy in (2, 1, 3):
            wait = 3 if dz % 2 == 1 and dy == 2 else Y_WAIT[dz]
            give(layer, dz, half, gy_sem.at[layer, wait], y_peers[dy])

    def take_y(layer, wait, blocks):
        await_into(helds[layer].at[pl.ds(0, blocks)], gy_sem.at[layer, wait])

    def gather_give(layer, half):
        ahead = 1 if half == 0 else 3
        give_z(layer, 0, half, ahead)
        give_z(layer, 0, half, 4 - ahead)
        spread(layer, 0, half)
        if layer > 0 and half == 1:
            give_z(layer, 0, 0, 2)
            give_z(layer, 0, 1, 2)

    def gather_take(layer):
        for dz, half, step in ((3, 0, 1), (1, 1, 3), (1, 0, 0), (3, 1, 0)):
            take_z(layer, dz, half)
            if layer == 0 and step > 0:
                give_z(layer, dz, half, step)
            spread(layer, dz, half)
        if layer == 0:
            hear_near(1)
            tell_near(2)
        else:
            settle(layer - 1, (3, 4))
        take_y(layer, 0, 3)
        multiply(layer, [((0, 0), (0, 1)), ((0, 2), (0, 3))], True)
        for half in (0, 1):
            take_z(layer, 2, half)
            spread(layer, 2, half)
        multiply(layer, [((3, 0), (1, 0))], False)
        take_y(layer, 1, 4)
        multiply(layer, [((3, 1), (3, 3)), ((1, 1), (1, 3))], False)
        take_y(layer, 3, 2)
        multiply(layer, [((3, 2), (1, 2))], False)
        take_y(layer, 2, 3)

    def products(layer, groups, block):
        held = helds[layer]
        total = None
        for group in groups:
            origins = [at_row(*step) for step in group]
            slots = [table_s[block // 8, block % 8 * ROWS + origin] for origin in origins]
            left = jnp.concatenate([merged[slot] for slot in slots], axis=1)
            right = jnp.concatenate([held[origin] for origin in origins], axis=0)
            term = jnp.dot(left, right, preferred_element_type=jnp.float32)
            total = term if total is None else total + term
        return total

    def multiply(layer, groups, fresh):
        def step(at, carry):
            for inner in range(16):
                block = at * 16 + inner
                total = products(layer, groups, block)
                totals[block] = total if fresh else totals[block] + total
            return carry

        lax.fori_loop(0, COLS // 16, step, 0)

    def complete(layer, dz, dx, other):
        block = at_col(dz, dx, other)
        return totals[block] + products(layer, LAST, block)

    def own(layer, half, dz, dx):
        from_sibling = recv_c[layer, dz, half, dx].astype(jnp.float32)
        return totals[at_col(dz, dx, False), pl.ds(half * HALF, HALF)] + from_sibling

    def stage_core(layer, dz):
        for dx in DX_ORDER:
            whole = complete(layer, dz, dx, True).astype(jnp.bfloat16)
            send_c[layer, dz, 0, dx] = whole[:HALF]
            send_c[layer, dz, 1, dx] = whole[HALF:]
        at = (layer, dz)
        push(send_c.at[at], recv_c.at[at], sent_sem.at[layer, 1], cr_sem.at[at], sibling)

    def stage_far(layer, half, dz):
        for dx in DX_ORDER:
            if (half, dz) in SUMMED:
                if dx > 0:
                    at = (layer, SUMMED.index((half, dz)))
                    send_a[*at, dx - 1] = own(layer, half, dz, dx).astype(jnp.bfloat16)
                    push(
                        send_a.at[*at, dx - 1], recv_a.at[*at, dx - 1],
                        sent_sem.at[layer, 5 if at[1] < 2 else 2], ar_sem.at[at], peers[0, dx],
                    )
            elif (dz, dx) != (0, 0):
                at = (layer, 4 * DIRECT.index(dz) + dx - 1)
                send_b[at] = own(layer, 1, dz, dx).astype(jnp.bfloat16)
                push(
                    send_b.at[at], recv_b.at[at],
                    sent_sem.at[layer, 3], br_sem.at[layer], peers[dz, dx],
                )

    def stage_mine(layer, half, dz):
        at = (layer, SUMMED.index((half, dz)))
        await_into(recv_a.at[at], ar_sem.at[at])
        whole = own(layer, half, dz, 0)
        for dx in range(3):
            whole = whole + recv_a[*at, dx].astype(jnp.float32)
        if dz > 0:
            send_z[at] = whole.astype(jnp.bfloat16)
            push(send_z.at[at], recv_z.at[at], sent_sem.at[layer, 4], zr_sem.at[layer], peers[dz, 0])
        return whole

    def finish(layer, half, whole):
        hidden = jnp.dot(
            whole.astype(jnp.bfloat16), weight_v[layer], preferred_element_type=jnp.float32
        )
        span = pl.ds(half * HALF, HALF)
        if layer + 1 < LAYERS:
            helds[layer + 1][row, span] = jnp.maximum(hidden, 0.0).astype(jnp.bfloat16)
            gather_give(layer + 1, half)
        else:
            out_ref[span] = hidden.astype(jnp.bfloat16)

    for half in (0, 1):
        gather_give(0, half)
    tell_near(0)
    sort_slots()
    hear_near(0)
    tell_near(1)
    for layer in range(LAYERS):
        gather_take(layer)
        for dz in DZ_ORDER:
            stage_core(layer, dz)
        if layer == 0:
            hear_near(2)
        for half, dz in CHUNKS:
            if half == 0:
                for dx in DX_ORDER:
                    totals[at_col(dz, dx, False)] = complete(layer, dz, dx, False)
                await_into(recv_c.at[layer, dz], cr_sem.at[layer, dz])
            if (half, dz) == (1, 1):
                await_sent(send_a.at[layer, pl.ds(0, 2)], sent_sem.at[layer, 5])
            stage_far(layer, half, dz)
        for half, dz in SUMMED:
            upper = stage_mine(layer, half, dz)
        settle(layer, (0, 1, 2))
        await_into(recv_z.at[layer], zr_sem.at[layer])
        for at, (half, dz) in enumerate(SUMMED):
            if half == 0 and dz > 0:
                upper = upper + recv_z[layer, at].astype(jnp.float32)
        finish(layer, 0, upper)
        await_into(recv_b.at[layer], br_sem.at[layer])
        lower = own(layer, 1, 0, 0)
        for at in range(11):
            lower = lower + recv_b[layer, at].astype(jnp.float32)
        lower = lower + recv_z[layer, SUMMED.index((1, 2))].astype(jnp.float32)
        finish(layer, 1, lower)

    settle(LAYERS - 1, (3, 4))


def shards(features, adjacency, block_rows, block_cols, counts, weights):
    bf16 = jnp.bfloat16
    out = pl.pallas_call(
        kernel,
        out_shape=jax.ShapeDtypeStruct((BLOCK, BLOCK), bf16),
        in_specs=[pl.BlockSpec(memory_space=pltpu.HBM)] * 6,
        out_specs=pl.BlockSpec(memory_space=pltpu.VMEM),
        scratch_shapes=[
            pltpu.VMEM((BLOCK, BLOCK, BLOCK), bf16),
            pltpu.VMEM((1, BLOCK), jnp.int32),
            pltpu.VMEM((1, BLOCK), jnp.int32),
            pltpu.VMEM((1, 1), jnp.int32),
            pltpu.VMEM((LAYERS, BLOCK, BLOCK), bf16),
            pltpu.VMEM((ROWS, BLOCK, BLOCK), bf16),
            pltpu.VMEM((ROWS, BLOCK, BLOCK), bf16),
            pltpu.VMEM((SLOTS + 1, BLOCK, BLOCK), jnp.float32),
            pltpu.VMEM((SLOTS + 1, BLOCK, BLOCK), bf16),
            pltpu.VMEM((COLS, BLOCK, BLOCK), jnp.float32),
            pltpu.VMEM((8, BLOCK), jnp.int32),
            pltpu.SMEM((8, BLOCK), jnp.int32),
            pltpu.VMEM((LAYERS, 4, 2, 4, HALF, BLOCK), bf16),
            pltpu.VMEM((LAYERS, 4, 2, 4, HALF, BLOCK), bf16),
            pltpu.VMEM((LAYERS, 5, 3, HALF, BLOCK), bf16),
            pltpu.VMEM((LAYERS, 5, 3, HALF, BLOCK), bf16),
            pltpu.VMEM((LAYERS, 11, HALF, BLOCK), bf16),
            pltpu.VMEM((LAYERS, 11, HALF, BLOCK), bf16),
            pltpu.VMEM((LAYERS, 4, HALF, BLOCK), bf16),
            pltpu.VMEM((LAYERS, 4, HALF, BLOCK), bf16),
            pltpu.SemaphoreType.DMA((7,)),
            pltpu.SemaphoreType.DMA((LAYERS, 6)),
            pltpu.SemaphoreType.DMA((LAYERS, 6)),
            pltpu.SemaphoreType.DMA((LAYERS, 4)),
            pltpu.SemaphoreType.DMA((LAYERS, 4)),
            pltpu.SemaphoreType.DMA((LAYERS, 5)),
            pltpu.SemaphoreType.DMA((LAYERS,)),
            pltpu.SemaphoreType.DMA((LAYERS,)),
            pltpu.SemaphoreType.REGULAR((3,)),
        ],
        compiler_params=pltpu.CompilerParams(
            collective_id=0, has_side_effects=True, vmem_limit_bytes=63 * 1024 * 1024
        ),
        cost_estimate=pl.CostEstimate(
            flops=2 * LAYERS * ROWS * COLS * BLOCK**3, bytes_accessed=2 * BLOCK**3, transcendentals=0
        ),
    )(features[0, 0], adjacency[0, 0], block_rows[0], block_cols[0], counts, weights)
    return out[None, None]


def solution(mesh):
    placed = (
        P("row", "col", None, None),
        P("row", "col", None, None, None),
        P("row", "col", None),
        P("row", "col", None),
        P("row", "col"),
        P(),
    )
    return jax.shard_map(
        shards, mesh=mesh, in_specs=placed, out_specs=P("row", "col", None, None), check_vma=False
    )
```
